32 devices in a mesh: parts: 2 (over x), tm: 16 (over z, y, core).
Axes of the slice: x: 2, y: 2, z: 4, core: 2. Of those that a mesh axis runs over, the one named last changes fastest.
Arguments:
- query_states: bfloat16 [32, 384, 768], P(('parts', 'tm')), parts along dimension 0, may hold values from -88 to 88
- key_states: bfloat16 [32, 384, 768], P(('parts', 'tm')), parts along dimension 0, may hold values from -4 to 4
- value_states: bfloat16 [32, 384, 768], P(('parts', 'tm')), parts along dimension 0, may hold values from -40 to 40
- out_weight: bfloat16 [1536, 3072], replicated, may hold values from -0.15625 to 0.15625
Outputs:
- mixed: bfloat16 [6144, 3072], P(('parts', 'tm')), parts along dimension 0
The draws below stay inside these ranges and needn't reach their ends.
There are 2 independent parts, one for each index of `parts`. The reference program is written for one: setup_inputs(seed, part) draws one part's arguments, and reference() takes and returns one part's arrays. A program takes and returns all parts, laid end to end along the dimension named above; an argument that names none is the same for every part. Nothing has to cross between parts.
All inputs are finite; a program needn't handle non-finite values.
Results may differ from the reference program's by a relative error of at most 0.0058.
Values may be sent and summed in bfloat16 or wider, within the bound.
No kernel may reach another device: no remote copies, remote signals or barrier semaphores. Data moves between devices by JAX's collectives and lax.ppermute only.
A program may use at most 128 MiB of HBM per device.

```python
import jax
import jax.numpy as jnp
from jax import lax

TCOLS = 4
HEADS = 12
HD = 128
D = 3072
TOK_DEV = 384
TILES = 8
T_TILES = 2
TOKENS = 3072


def to_blocks(grid):
    half_width = grid.shape[2] // 2
    return grid.reshape(TILES, TOK_DEV, 2, half_width).transpose(0, 2, 1, 3).reshape(2 * TILES, TOK_DEV, half_width)


def key_grid(key):
    normal_draw = jax.random.normal(jax.random.fold_in(key, 7), (TILES, TOK_DEV, HEADS * HD), jnp.float32)
    values_out = jnp.clip(normal_draw, -4.0, 4.0)
    sign_draw = jnp.where(jax.random.bernoulli(jax.random.fold_in(key, 13), 0.5, (TILES,)), 4.0, -4.0)
    last_col = HEADS * HD - 1
    pick_row = 5 % TOK_DEV
    values_out = values_out.at[:, pick_row, last_col].set(sign_draw)
    values_out = values_out.at[:, pick_row, last_col - 1].set(-sign_draw)
    return values_out


def draw_key_states(key, part):
    values_out = key_grid(key)
    return to_blocks(values_out).astype(jnp.bfloat16)


def draw_query_states(key, part):
    normal_draw = jax.random.normal(jax.random.fold_in(key, 3), (TILES, TOK_DEV, HEADS * HD), jnp.float32)
    values_out = jnp.clip(normal_draw, -4.0, 4.0)
    return to_blocks(values_out).astype(jnp.bfloat16)


def shard_levels(stream_key, shape, cuts, low, high):
    level = 1.0
    for position, blocks in cuts:
        draws = jax.random.uniform(jax.random.fold_in(jax.random.fold_in(stream_key, 6), position), (blocks,), jnp.float32, low / len(cuts), high / len(cuts))
        level = level * jnp.repeat(jnp.exp(draws), shape[position] // blocks).reshape((-1,) + (1,) * (len(shape) - 1 - position))
    return level


def gaussian(key, dims, scale, most, cuts=(), held_as=jnp.bfloat16):
    loudness = shard_levels(key, dims, cuts, -0.22, 0.18) if cuts else 1.0
    values = jax.random.normal(key, dims, jnp.float32) * scale * loudness
    return jnp.minimum(jnp.maximum(values, -most), most).astype(held_as)


def setup_inputs(seed: int = 0, part: int = 0) -> dict:
    seeds = jax.random.split(jax.random.key(seed), 5)
    own_keys = jax.random.split(jax.random.fold_in(seeds[4], part), 5)
    query_states = draw_query_states(jax.random.fold_in(jax.random.fold_in(seeds[4], part), 71), part)
    key_states = draw_key_states(jax.random.fold_in(jax.random.fold_in(seeds[4], part), 71), part)
    value_states = gaussian(own_keys[2], (2 * TILES, TOK_DEV, HEADS * HD // 2), 8.0, 40.0, ((0, 16),))
    out_weight = gaussian(seeds[3], (HEADS * HD, D), (HEADS * HD) ** -0.5, 0.15625)
    return {"query_states": query_states, "key_states": key_states, "value_states": value_states, "out_weight": out_weight}


masked_score = -1e30


def to_tiles(blocks):
    tile_count = blocks.shape[0] // 2
    half_width = blocks.shape[2]
    return blocks.reshape(tile_count, 2, TOK_DEV, half_width).transpose(0, 2, 1, 3).reshape(tile_count, TOK_DEV, 2 * half_width)


def tile_attention(query_tile, key_window, value_window, key_ok):
    score_scale = HD ** -0.5
    pieces = []
    for head_index in range(HEADS):
        first_col = head_index * HD
        query_head = query_tile[:, first_col:first_col + HD]
        key_head = key_window[:, first_col:first_col + HD]
        value_head = value_window[:, first_col:first_col + HD]
        scores = lax.dot_general(query_head, key_head, (((1,), (1,)), ((), ())), preferred_element_type=jnp.float32) * score_scale
        scores = jnp.where(key_ok[None, :], scores, masked_score)
        row_max = jnp.max(scores, axis=1, keepdims=True)
        exp_scores = jnp.exp(scores - row_max)
        denominator = jnp.sum(exp_scores, axis=1, keepdims=True)
        weights = (exp_scores / denominator).astype(jnp.bfloat16)
        pieces.append(jnp.dot(weights, value_head, preferred_element_type=jnp.float32).astype(jnp.bfloat16))
    return jnp.concatenate(pieces, axis=1)


def reference(query_states, key_states, value_states, out_weight):
    width_all = HEADS * HD
    query_tiles = to_tiles(query_states)
    key_layout = to_tiles(key_states).reshape(T_TILES, TCOLS, TOK_DEV, width_all)
    value_layout = to_tiles(value_states).reshape(T_TILES, TCOLS, TOK_DEV, width_all)
    border = ((1, 1), (1, 1), (0, 0), (0, 0))
    key_padded = jnp.pad(key_layout, border)
    value_padded = jnp.pad(value_layout, border)
    tile_steps = jnp.arange(3, dtype=jnp.int32) - 1
    zero_index = jnp.zeros((), jnp.int32)

    def one_tile(tile_index):
        time_tile = (tile_index // TCOLS).astype(jnp.int32)
        col_tile = (tile_index % TCOLS).astype(jnp.int32)
        starts = (time_tile, col_tile, zero_index, zero_index)
        window_shape = (3, 3, TOK_DEV, width_all)
        key_window = lax.dynamic_slice(key_padded, starts, window_shape).reshape(9 * TOK_DEV, width_all)
        value_window = lax.dynamic_slice(value_padded, starts, window_shape).reshape(9 * TOK_DEV, width_all)
        time_ok = (time_tile + tile_steps >= 0) & (time_tile + tile_steps < T_TILES)
        col_ok = (col_tile + tile_steps >= 0) & (col_tile + tile_steps < TCOLS)
        tile_ok = (time_ok[:, None] & col_ok[None, :]).reshape(9)
        key_ok = jnp.repeat(tile_ok, TOK_DEV)
        query_tile = lax.dynamic_index_in_dim(query_tiles, tile_index, 0, keepdims=False)
        return tile_attention(query_tile, key_window, value_window, key_ok)

    attended = lax.map(one_tile, jnp.arange(TILES, dtype=jnp.int32)).reshape(TOKENS, width_all)
    mixed_rows = jnp.dot(attended, out_weight, preferred_element_type=jnp.float32)
    return mixed_rows.astype(jnp.bfloat16)
```

```python
import functools
import math

import jax
import jax.numpy as jnp
from jax import lax
from jax.experimental import pallas as pl
from jax.experimental.pallas import tpu as pltpu
from jax.sharding import PartitionSpec as P

TCOLS = 4
HD = 128
CHUNK_HEADS = 2
STAT_ROWS = 16
EXP2_SCALE = HD ** (-0.5) * math.log2(math.e)
MASKED = -1e30
VMEM_BYTES = 48 * 1024 * 1024


def dot_rows(a, b):
    return lax.dot_general(a, b, (((1,), (1,)), ((), ())), preferred_element_type=jnp.float32)


def attend_kernel(q_ref, own_ref, next_ref, far_ref, same_ref, cross_ref):
    position = lax.axis_index("tm")
    group = position % 2
    col = (position // 2) % TCOLS
    far_ok = (col == 1) | (col == 2)
    rows = q_ref.shape[0]
    half = rows // 2
    width = q_ref.shape[1]
    stats = []
    outs = []
    for head in range(width // HD):
        cols = slice(head * HD, (head + 1) * HD)
        query = q_ref[:, cols]
        s_own = dot_rows(own_ref[0, :, cols], query)
        s_next = dot_rows(next_ref[0, :, cols], query)
        s_far = dot_rows(far_ref[0, :, cols], query)
        s_far = jnp.where(far_ok, s_far, MASKED)
        top = jnp.maximum(jnp.maximum(s_own, s_next), s_far)
        top = jnp.max(top, axis=0, keepdims=True).astype(jnp.bfloat16).astype(jnp.float32)
        total = jnp.zeros((1, rows), jnp.float32)
        out = jnp.zeros((HD, rows), jnp.float32)
        for scores, ref in ((s_own, own_ref), (s_next, next_ref), (s_far, far_ref)):
            probs = jnp.exp2((scores - top) * EXP2_SCALE)
            total += jnp.sum(probs, axis=0, keepdims=True)
            out += lax.dot_general(
                ref[1, :, cols],
                probs.astype(jnp.bfloat16),
                (((0,), (0,)), ((), ())),
                preferred_element_type=jnp.float32,
            )
        high = total.astype(jnp.bfloat16).astype(jnp.float32)
        stats += [top, high, total - high]
        outs.append(out.T.astype(jnp.bfloat16))
    stats.append(jnp.zeros((STAT_ROWS - len(stats), rows), jnp.float32))
    stats = jnp.concatenate(stats, axis=0).astype(jnp.bfloat16)
    out = jnp.concatenate(outs, axis=1)

    def put(ref, part):
        ref[:half, :] = out[part * half : (part + 1) * half]
        first = part * (rows - width)
        ref[half:, :] = stats[:, first : first + width]

    @pl.when(group == 0)
    def _():
        put(same_ref, 0)
        put(cross_ref, 1)

    @pl.when(group == 1)
    def _():
        put(same_ref, 1)
        put(cross_ref, 0)


def attend(query, own, nxt, far):
    rows, width = query.shape
    keys = 3 * own.shape[1]
    out = jax.ShapeDtypeStruct((rows // 2 + STAT_ROWS, width), jnp.bfloat16)
    return pl.pallas_call(
        attend_kernel,
        out_shape=(out, out),
        compiler_params=pltpu.CompilerParams(vmem_limit_bytes=VMEM_BYTES),
        cost_estimate=pl.CostEstimate(
            flops=4 * rows * keys * width,
            bytes_accessed=2 * width * (2 * rows + 2 * keys),
            transcendentals=rows * keys * width // HD,
        ),
        name="attend",
    )(query, own, nxt, far)


def merge(refs, oks, half, width, part):
    shift = width - half
    parts = []
    for ref, ok in zip(refs, oks):
        stats = ref[half:, :].astype(jnp.float32).T
        stats = jnp.where(part == 0, stats[:half], stats[shift:])
        parts.append((ref[:half, :].astype(jnp.float32), stats, ok))
    heads = []
    for head in range(width // HD):
        cols = slice(head * HD, (head + 1) * HD)
        tops, sums = [], []
        for _, stats, ok in parts:
            top = stats[:, 3 * head : 3 * head + 1]
            tops.append(top if ok is None else jnp.where(ok, top, MASKED))
            sums.append(stats[:, 3 * head + 1 : 3 * head + 2] + stats[:, 3 * head + 2 : 3 * head + 3])
        top = functools.reduce(jnp.maximum, tops)
        weights = [jnp.exp2((t - top) * EXP2_SCALE) for t in tops]
        total = sum(w * s for w, s in zip(weights, sums))
        value = sum(w * p[0][:, cols] for w, p in zip(weights, parts))
        heads.append((value / total).astype(jnp.bfloat16))
    return jnp.concatenate(heads, axis=1)


def project_kernel(steps, time_count, has_total, *refs):
    count = len(steps) + 1
    mine, other = refs[:count], refs[count : 2 * count]
    w_ref = refs[2 * count]
    total_ref = refs[2 * count + 1] if has_total else None
    out_ref, held = refs[-2:]
    position = lax.axis_index("tm")
    group = position % 2
    time_tile = position // (2 * TCOLS)
    width = held.shape[2]
    half = held.shape[1]

    @pl.when(pl.program_id(0) == 0)
    def _():
        oks = [None]
        for step in steps:
            source = time_tile + step
            oks.append(None if time_count == 2 else (source >= 0) & (source < time_count))
        held[0] = merge(mine, oks, half, width, group)
        held[1] = merge(other, oks, half, width, group)

    result = jnp.dot(held[0], w_ref[group], preferred_element_type=jnp.float32)
    result += jnp.dot(held[1], w_ref[1 - group], preferred_element_type=jnp.float32)
    if has_total:
        result += total_ref[...]
    out_ref[...] = result.astype(out_ref.dtype)


def project(mine, other, weight, chunk, total, steps, time_count, dtype):
    tall, width = mine[0].shape
    half = tall - STAT_ROWS
    model = weight.shape[2]
    block = 512 if model % 512 == 0 else model
    whole = pl.BlockSpec((tall, width), lambda n: (0, 0))
    tile = pl.BlockSpec((half, block), lambda n: (0, n))
    in_specs = [whole] * (2 * len(mine)) + [pl.BlockSpec((2, width, block), lambda n: (0, chunk, n))]
    args = [*mine, *other, weight]
    if total is not None:
        in_specs.append(tile)
        args.append(total)
    return pl.pallas_call(
        functools.partial(project_kernel, steps, time_count, total is not None),
        grid=(model // block,),
        in_specs=in_specs,
        out_specs=tile,
        out_shape=jax.ShapeDtypeStruct((half, model), dtype),
        scratch_shapes=[pltpu.VMEM((2, half, width), jnp.bfloat16)],
        compiler_params=pltpu.CompilerParams(vmem_limit_bytes=VMEM_BYTES),
        cost_estimate=pl.CostEstimate(
            flops=4 * half * width * model,
            bytes_accessed=4 * width * model + 4 * half * model,
            transcendentals=0,
        ),
        name="project",
    )(*args)


def per_device(query_states, key_states, value_states, out_weight):
    query, key, value = query_states[0], key_states[0], value_states[0]
    half_width = query.shape[1]
    devices = lax.axis_size("tm")
    time_count = devices // (2 * TCOLS)
    places = range(devices)
    row = 2 * TCOLS
    width = CHUNK_HEADS * HD
    chunks = half_width // width

    next_route = [(p, p ^ 2) for p in places]
    far_route = [(p, p ^ 4) for p in places if (p // 2) % TCOLS in (0, 3)]
    if time_count == 2:
        steps = (1,)
        ask_routes = [[(p, p ^ row) for p in places]]
    else:
        steps = (1, -1)
        ask_routes = [[(p, p + s * row) for p in places if 0 <= p + s * row < devices] for s in steps]
    same_routes = [[(b, a) for a, b in route] for route in ask_routes]
    cross_routes = [[(b, a ^ 1) for a, b in route] for route in ask_routes]
    core_route = [(p, p ^ 1) for p in places]

    weight = out_weight.reshape(2, half_width, out_weight.shape[1])
    cuts = [slice(c * width, (c + 1) * width) for c in range(chunks)]
    total = None
    for c in range(chunks):
        q_part = query[:, cuts[c]]
        asked = [lax.ppermute(q_part, "tm", route) for route in ask_routes]
        own = jnp.stack((key[:, cuts[c]], value[:, cuts[c]]))
        nxt = lax.ppermute(own, "tm", next_route)
        far = lax.ppermute(nxt, "tm", far_route)
        mine, other = [], []
        for q, same_route, cross_route in zip(asked, same_routes, cross_routes):
            same, cross = attend(q, own, nxt, far)
            mine.append(lax.ppermute(same, "tm", same_route))
            other.append(lax.ppermute(cross, "tm", cross_route))
        same, cross = attend(q_part, own, nxt, far)
        mine.insert(0, same)
        other.insert(0, lax.ppermute(cross, "tm", core_route))
        last = c == chunks - 1
        total = project(
            mine, other, weight, c, total, steps, time_count, jnp.bfloat16 if last else jnp.float32
        )
    return total


def solution(mesh):
    in_specs = (
        P(("parts", "tm"), None, None),
        P(("parts", "tm"), None, None),
        P(("parts", "tm"), None, None),
        P(),
    )
    out_specs = P(("parts", "tm"), None)
    return jax.shard_map(
        per_device, mesh=mesh, in_specs=in_specs, out_specs=out_specs, check_vma=False
    )
```

```python
import functools
import math

import jax
import jax.numpy as jnp
from jax import lax
from jax.experimental import pallas as pl
from jax.experimental.pallas import tpu as pltpu
from jax.sharding import PartitionSpec as P

TCOLS = 4
HD = 128
CHUNK_HEADS = 2
STAT_ROWS = 16
EXP2_SCALE = HD ** (-0.5) * math.log2(math.e)
MASKED = -1e30
VMEM_BYTES = 32 * 1024 * 1024


def after(array, *earlier):
    return lax.optimization_barrier((array, *earlier))[0]


def dot_rows(a, b):
    return lax.dot_general(a, b, (((1,), (1,)), ((), ())), preferred_element_type=jnp.float32)


def stat_blocks(rows, width):
    return -(-rows // width)


def attend_kernel(q_ref, own_ref, next_ref, far_ref, out_ref):
    col = (lax.axis_index("tm") // 2) % TCOLS
    far_ok = (col == 1) | (col == 2)
    rows, width = q_ref.shape
    stats = []
    for head in range(width // HD):
        cols = slice(head * HD, (head + 1) * HD)
        query = q_ref[:, cols]
        s_own = dot_rows(own_ref[0, :, cols], query)
        s_next = dot_rows(next_ref[0, :, cols], query)
        s_far = dot_rows(far_ref[0, :, cols], query)
        s_far = jnp.where(far_ok, s_far, MASKED)
        top = jnp.maximum(jnp.maximum(s_own, s_next), s_far)
        top = jnp.max(top, axis=0, keepdims=True).astype(jnp.bfloat16).astype(jnp.float32)
        total = jnp.zeros((1, rows), jnp.float32)
        out = jnp.zeros((HD, rows), jnp.float32)
        for scores, ref in ((s_own, own_ref), (s_next, next_ref), (s_far, far_ref)):
            probs = jnp.exp2((scores - top) * EXP2_SCALE).astype(jnp.bfloat16)
            total += jnp.sum(probs.astype(jnp.float32), axis=0, keepdims=True)
            out += lax.dot_general(
                ref[1, :, cols],
                probs,
                (((0,), (0,)), ((), ())),
                preferred_element_type=jnp.float32,
            )
        high = total.astype(jnp.bfloat16).astype(jnp.float32)
        stats += [top, high, total - high]
        out_ref[:rows, cols] = out.T.astype(out_ref.dtype)
    stats.append(jnp.zeros((STAT_ROWS - len(stats), rows), jnp.float32))
    stats = jnp.concatenate(stats, axis=0)
    for block in range(stat_blocks(rows, width)):
        piece = stats[:, block * width : (block + 1) * width]
        if piece.shape[1] < width:
            piece = jnp.concatenate(
                (piece, jnp.zeros((STAT_ROWS, width - piece.shape[1]), jnp.float32)), axis=1
            )
        first = rows + block * STAT_ROWS
        out_ref[first : first + STAT_ROWS, :] = piece.astype(out_ref.dtype)


def attend(query, own, nxt, far, dtype):
    rows, width = query.shape
    keys = 3 * own.shape[1]
    return pl.pallas_call(
        attend_kernel,
        out_shape=jax.ShapeDtypeStruct((rows + STAT_ROWS * stat_blocks(rows, width), width), dtype),
        compiler_params=pltpu.CompilerParams(vmem_limit_bytes=VMEM_BYTES),
        cost_estimate=pl.CostEstimate(
            flops=4 * rows * keys * width,
            bytes_accessed=2 * width * (2 * rows + 2 * keys),
            transcendentals=rows * keys * width // HD,
        ),
        name="attend",
    )(query, own, nxt, far)


def join_kernel(steps, time_count, *refs):
    mine_ref, other_ref = refs[-2:]
    half, width = mine_ref.shape
    rows = 2 * half
    position = lax.axis_index("tm")
    group = position % 2
    time_tile = position // (2 * TCOLS)
    parts = []
    for ref, step in zip(refs, (0, *steps)):
        source = time_tile + step
        ok = None if step == 0 or time_count == 2 else (source >= 0) & (source < time_count)
        stats = [
            ref[rows + block * STAT_ROWS : rows + (block + 1) * STAT_ROWS, :].astype(jnp.float32)
            for block in range(stat_blocks(rows, width))
        ]
        stats = jnp.concatenate(stats, axis=1)[:, :rows].T
        parts.append((ref, stats, ok))
    for head in range(width // HD):
        cols = slice(head * HD, (head + 1) * HD)
        tops, sums = [], []
        for _, stats, ok in parts:
            top = stats[:, 3 * head : 3 * head + 1]
            tops.append(top if ok is None else jnp.where(ok, top, MASKED))
            sums.append(stats[:, 3 * head + 1 : 3 * head + 2] + stats[:, 3 * head + 2 : 3 * head + 3])
        top = functools.reduce(jnp.maximum, tops)
        weights = [jnp.exp2((t - top) * EXP2_SCALE) for t in tops]
        inverse = 1.0 / sum(w * s for w, s in zip(weights, sums))
        value = sum((w * inverse) * p[0][:rows, cols].astype(jnp.float32) for w, p in zip(weights, parts))
        value = value.astype(jnp.bfloat16)
        mine_ref[:, cols] = jnp.where(group == 0, value[:half], value[half:])
        other_ref[:, cols] = jnp.where(group == 0, value[half:], value[:half])


def join(parts, rows, steps, time_count):
    width = parts[0].shape[1]
    out = jax.ShapeDtypeStruct((rows // 2, width), jnp.bfloat16)
    return pl.pallas_call(
        functools.partial(join_kernel, steps, time_count),
        out_shape=(out, out),
        compiler_params=pltpu.CompilerParams(vmem_limit_bytes=VMEM_BYTES),
        cost_estimate=pl.CostEstimate(
            flops=8 * rows * width, bytes_accessed=10 * rows * width, transcendentals=0
        ),
        name="join",
    )(*parts)


def project_kernel(first, swaps, has_total, *refs):
    inputs, w_ref, out_ref = refs[: len(swaps)], refs[len(swaps)], refs[-1]
    group = lax.axis_index("tm") % 2
    width = inputs[0].shape[1]
    model = w_ref.shape[2]
    block = 512 if model % 512 == 0 else model
    for start in range(0, model, block):
        cols = slice(start, start + block)
        result = refs[len(swaps) + 1][:, cols] if has_total else 0.0
        for ref, swap in zip(inputs, swaps):
            which = 1 - group if swap else group
            result += jnp.dot(
                ref[...], w_ref[which, first : first + width, cols], preferred_element_type=jnp.float32
            )
        out_ref[:, cols] = result.astype(out_ref.dtype)


def project(inputs, swaps, weight, first, total, dtype):
    half, width = inputs[0].shape
    model = weight.shape[2]
    args = [*inputs, weight] if total is None else [*inputs, weight, total]
    return pl.pallas_call(
        functools.partial(project_kernel, first, swaps, total is not None),
        in_specs=[pl.BlockSpec(memory_space=pltpu.VMEM)] * len(args),
        out_specs=pl.BlockSpec(memory_space=pltpu.VMEM),
        out_shape=jax.ShapeDtypeStruct((half, model), dtype),
        compiler_params=pltpu.CompilerParams(vmem_limit_bytes=VMEM_BYTES),
        cost_estimate=pl.CostEstimate(
            flops=2 * len(inputs) * half * width * model,
            bytes_accessed=2 * len(inputs) * width * model + 4 * half * model,
            transcendentals=0,
        ),
        name="project",
    )(*args)


def per_device(query_states, key_states, value_states, out_weight):
    query, key, value = query_states[0], key_states[0], value_states[0]
    half_width = query.shape[1]
    devices = lax.axis_size("tm")
    time_count = devices // (2 * TCOLS)
    places = range(devices)
    row = 2 * TCOLS
    width = CHUNK_HEADS * HD
    chunks = half_width // width

    next_route = [(p, p ^ 2) for p in places]
    far_route = [(p, p ^ 4) for p in places if (p // 2) % TCOLS in (0, 3)]
    across_route = [(p, p ^ 6) for p in places if (p // 2) % TCOLS in (1, 2)]
    if time_count == 2:
        steps = (1,)
        ask_routes = [[(p, p ^ row) for p in places]]
    else:
        steps = (1, -1)
        ask_routes = [[(p, p + s * row) for p in places if 0 <= p + s * row < devices] for s in steps]
    back_routes = [[(b, a) for a, b in route] for route in ask_routes]
    core_route = [(p, p ^ 1) for p in places]

    weight = out_weight.reshape(2, half_width, out_weight.shape[1])
    cuts = [slice(c * width, (c + 1) * width) for c in range(chunks)]
    q_parts = [query[:, cut] for cut in cuts]
    kv_parts = [jnp.stack((key[:, cuts[0]], value[:, cuts[0]]))]
    key, value = after((key, value), kv_parts[0])
    kv_parts += [jnp.stack((key[:, cut], value[:, cut])) for cut in cuts[1:]]
    asked_all = [lax.ppermute(query, "tm", route) for route in ask_routes]
    asked = [[q[:, cut] for q in asked_all] for cut in cuts]
    nexts, fars = [], []
    for c in range(chunks):
        kv_part = after(kv_parts[c], nexts[0]) if c == chunks - 1 else kv_parts[c]
        nexts.append(lax.ppermute(kv_part, "tm", next_route))
        if c < chunks - 1:
            fars.append(lax.ppermute(after(nexts[c], *asked_all) if c else nexts[c], "tm", far_route))
        else:
            fars.append(lax.ppermute(kv_part, "tm", across_route))
    total = None
    owns, backs = [], []
    for c in range(chunks):
        keys = kv_parts[c], nexts[c], fars[c]
        remote = [attend(q, *keys, jnp.bfloat16) for q in asked[c]]
        backs.append([lax.ppermute(part, "tm", route) for part, route in zip(remote, back_routes)])
        owns.append(keys)
    owns = [attend(after(q_parts[c], *remote), *owns[c], jnp.float32) for c in range(chunks)]
    backs = [[after(back, *owns) for back in parts] for parts in backs]
    for c in range(chunks):
        mine, other = join((owns[c], *backs[c]), query.shape[0], steps, time_count)
        other = lax.ppermute(other, "tm", core_route)
        if c < chunks - 1:
            total = project((mine, other), (False, True), weight, cuts[c].start, total, jnp.float32)
        else:
            total = project((mine,), (False,), weight, cuts[c].start, total, jnp.float32)
            total = project((other,), (True,), weight, cuts[c].start, total, jnp.bfloat16)
    return total


def solution(mesh):
    in_specs = (
        P(("parts", "tm"), None, None),
        P(("parts", "tm"), None, None),
        P(("parts", "tm"), None, None),
        P(),
    )
    out_specs = P(("parts", "tm"), None)
    return jax.shard_map(
        per_device, mesh=mesh, in_specs=in_specs, out_specs=out_specs, check_vma=False
    )
```

```python
import functools
import math

import jax
import jax.numpy as jnp
from jax import lax
from jax.experimental import pallas as pl
from jax.experimental.pallas import tpu as pltpu
from jax.sharding import PartitionSpec as P

TCOLS = 4
HD = 128
CHUNK_HEADS = 2
STAT_ROWS = 16
EXP2_SCALE = HD ** (-0.5) * math.log2(math.e)
MASKED = -1e30
VMEM_BYTES = 32 * 1024 * 1024


def after(array, *earlier):
    return lax.optimization_barrier((array, *earlier))[0]


def dot_rows(a, b):
    return lax.dot_general(a, b, (((1,), (1,)), ((), ())), preferred_element_type=jnp.float32)


def stat_blocks(rows, width):
    return -(-rows // width)


def is_edge():
    col = (lax.axis_index("tm") // 2) % TCOLS
    return (col == 0) | (col == TCOLS - 1)


def attend_tiles(q_ref, tiles, out_ref):
    rows, width = q_ref.shape
    stats = []
    for head in range(width // HD):
        cols = slice(head * HD, (head + 1) * HD)
        query = q_ref[:, cols]
        scores = [dot_rows(tile[0, :, cols], query) for tile in tiles]
        top = jnp.max(functools.reduce(jnp.maximum, scores), axis=0, keepdims=True)
        top = top.astype(jnp.bfloat16).astype(jnp.float32)
        total = jnp.zeros((1, rows), jnp.float32)
        out = jnp.zeros((HD, rows), jnp.float32)
        for score, tile in zip(scores, tiles):
            probs = jnp.exp2((score - top) * EXP2_SCALE).astype(jnp.bfloat16)
            total += jnp.sum(probs.astype(jnp.float32), axis=0, keepdims=True)
            out += lax.dot_general(
                tile[1, :, cols], probs, (((0,), (0,)), ((), ())), preferred_element_type=jnp.float32
            )
        high = total.astype(jnp.bfloat16).astype(jnp.float32)
        stats += [top, high, total - high]
        out_ref[:rows, cols] = out.T.astype(out_ref.dtype)
    stats.append(jnp.zeros((STAT_ROWS - len(stats), rows), jnp.float32))
    stats = jnp.concatenate(stats, axis=0)
    for block in range(stat_blocks(rows, width)):
        piece = stats[:, block * width : (block + 1) * width]
        if piece.shape[1] < width:
            piece = jnp.concatenate(
                (piece, jnp.zeros((STAT_ROWS, width - piece.shape[1]), jnp.float32)), axis=1
            )
        first = rows + block * STAT_ROWS
        out_ref[first : first + STAT_ROWS, :] = piece.astype(out_ref.dtype)


def attend_kernel(edges, inners, q_ref, *refs):
    tiles, out_ref = refs[:-1], refs[-1]
    edge = is_edge()
    if edges and inners:
        attend_tiles(q_ref, tiles, out_ref)
    elif edges:
        pl.when(edge)(lambda: attend_tiles(q_ref, tiles, out_ref))
    else:
        pl.when(jnp.logical_not(edge))(lambda: attend_tiles(q_ref, tiles, out_ref))


def attend(query, tiles, edges, inners, dtype, weight=1.0):
    rows, width = query.shape
    keys = len(tiles) * rows
    return pl.pallas_call(
        functools.partial(attend_kernel, edges, inners),
        out_shape=jax.ShapeDtypeStruct((rows + STAT_ROWS * stat_blocks(rows, width), width), dtype),
        compiler_params=pltpu.CompilerParams(vmem_limit_bytes=VMEM_BYTES),
        cost_estimate=pl.CostEstimate(
            flops=int(weight * 4 * rows * keys * width),
            bytes_accessed=int(weight * 2 * width * (2 * rows + 2 * keys)),
            transcendentals=int(weight * rows * keys * width // HD),
        ),
        name="attend",
    )(query, *tiles)


def join_kernel(steps, time_count, *refs):
    mine_ref, other_ref = refs[-2:]
    half, width = mine_ref.shape
    rows = 2 * half
    position = lax.axis_index("tm")
    group = position % 2
    time_tile = position // (2 * TCOLS)
    edge = is_edge()

    def load(ref, *index):
        at_edge, inner = ref
        inner = inner[index].astype(jnp.float32)
        return jnp.where(edge, 0.0 if at_edge is None else at_edge[index].astype(jnp.float32), inner)

    near, far = refs[:2]
    sources = [(near, near), (None, far)] + [refs[2 + 2 * n : 4 + 2 * n] for n in range(len(steps))]
    parts = []
    for ref, step in zip(sources, (0, 0, *steps)):
        source = time_tile + step
        ok = None if step == 0 or time_count == 2 else (source >= 0) & (source < time_count)
        if ref[0] is None:
            ok = jnp.logical_not(edge)
        stats = [
            load(ref, slice(rows + block * STAT_ROWS, rows + (block + 1) * STAT_ROWS), slice(None))
            for block in range(stat_blocks(rows, width))
        ]
        stats = jnp.concatenate(stats, axis=1)[:, :rows].T
        parts.append((ref, stats, ok))
    for head in range(width // HD):
        cols = slice(head * HD, (head + 1) * HD)
        tops, sums = [], []
        for _, stats, ok in parts:
            top = stats[:, 3 * head : 3 * head + 1]
            tops.append(top if ok is None else jnp.where(ok, top, MASKED))
            sums.append(stats[:, 3 * head + 1 : 3 * head + 2] + stats[:, 3 * head + 2 : 3 * head + 3])
        top = functools.reduce(jnp.maximum, tops)
        weights = [jnp.exp2((t - top) * EXP2_SCALE) for t in tops]
        inverse = 1.0 / sum(w * s for w, s in zip(weights, sums))
        value = sum((w * inverse) * load(p[0], slice(rows), cols) for w, p in zip(weights, parts))
        value = value.astype(jnp.bfloat16)
        mine_ref[:, cols] = jnp.where(group == 0, value[:half], value[half:])
        other_ref[:, cols] = jnp.where(group == 0, value[half:], value[:half])


def join(parts, rows, steps, time_count):
    width = parts[0].shape[1]
    out = jax.ShapeDtypeStruct((rows // 2, width), jnp.bfloat16)
    return pl.pallas_call(
        functools.partial(join_kernel, steps, time_count),
        out_shape=(out, out),
        compiler_params=pltpu.CompilerParams(vmem_limit_bytes=VMEM_BYTES),
        cost_estimate=pl.CostEstimate(
            flops=8 * rows * width, bytes_accessed=10 * rows * width, transcendentals=0
        ),
        name="join",
    )(*parts)


def project_kernel(first, swaps, has_total, *refs):
    inputs, w_ref, out_ref = refs[: len(swaps)], refs[len(swaps)], refs[-1]
    group = lax.axis_index("tm") % 2
    width = inputs[0].shape[1]
    model = w_ref.shape[2]
    block = 512 if model % 512 == 0 else model
    for start in range(0, model, block):
        cols = slice(start, start + block)
        result = refs[len(swaps) + 1][:, cols] if has_total else 0.0
        for ref, swap in zip(inputs, swaps):
            which = 1 - group if swap else group
            result += jnp.dot(
                ref[...], w_ref[which, first : first + width, cols], preferred_element_type=jnp.float32
            )
        out_ref[:, cols] = result.astype(out_ref.dtype)


def project(inputs, swaps, weight, first, total, dtype):
    half, width = inputs[0].shape
    model = weight.shape[2]
    args = [*inputs, weight] if total is None else [*inputs, weight, total]
    return pl.pallas_call(
        functools.partial(project_kernel, first, swaps, total is not None),
        in_specs=[pl.BlockSpec(memory_space=pltpu.VMEM)] * len(args),
        out_specs=pl.BlockSpec(memory_space=pltpu.VMEM),
        out_shape=jax.ShapeDtypeStruct((half, model), dtype),
        compiler_params=pltpu.CompilerParams(vmem_limit_bytes=VMEM_BYTES),
        cost_estimate=pl.CostEstimate(
            flops=2 * len(inputs) * half * width * model,
            bytes_accessed=2 * len(inputs) * width * model + 4 * half * model,
            transcendentals=0,
        ),
        name="project",
    )(*args)


def reverse(route):
    return [(b, a) for a, b in route]


def per_device(query_states, key_states, value_states, out_weight):
    query, key, value = query_states[0], key_states[0], value_states[0]
    rows, half_width = query.shape
    devices = lax.axis_size("tm")
    time_count = devices // (2 * TCOLS)
    places = range(devices)
    row = 2 * TCOLS

    def at_edge(place):
        return (place // 2) % TCOLS in (0, TCOLS - 1)

    next_route = [(p, p ^ 2) for p in places]
    far_route = [(p, p ^ 4) for p in places if at_edge(p)]
    across_route = [(p, p ^ 6) for p in places if not at_edge(p)]
    if time_count == 2:
        steps = (1,)
        ask_routes = [[(p, p ^ row) for p in places]]
    else:
        steps = (1, -1)
        ask_routes = [[(p, p + s * row) for p in places if 0 <= p + s * row < devices] for s in steps]
    edge_routes = [[pair for pair in route if at_edge(pair[0])] for route in ask_routes]
    inner_routes = [[pair for pair in route if not at_edge(pair[0])] for route in ask_routes]
    core_route = [(p, p ^ 1) for p in places]

    weight = out_weight.reshape(2, half_width, out_weight.shape[1])
    middle = half_width // HD // 2 * HD
    cuts = slice(0, middle), slice(middle, half_width)
    q_parts = [query[:, cut] for cut in cuts]
    own_0 = jnp.stack((key[:, cuts[0]], value[:, cuts[0]]))
    key, value = after((key, value), own_0)
    own_1 = jnp.stack((key[:, cuts[1]], value[:, cuts[1]]))

    edge_query = after(query, own_0)
    edge_asks = [lax.ppermute(edge_query, "tm", route) for route in edge_routes]
    next_0 = lax.ppermute(own_0, "tm", next_route)
    next_1 = lax.ppermute(own_1, "tm", next_route)
    inner_query = after(query, next_0)
    inner_asks = [lax.ppermute(inner_query, "tm", route) for route in inner_routes]
    far_0 = lax.ppermute(next_0, "tm", far_route)
    far_1 = lax.ppermute(after(own_1, next_0), "tm", across_route)
    tiles = (own_0, next_0, far_0), (own_1, next_1, far_1)

    def answer(asks, chunk, edges, earlier):
        near = tiles[chunk][:2] if edges else tiles[chunk]
        return [attend(after(q[:, cuts[chunk]], *earlier), near, edges, not edges, jnp.bfloat16) for q in asks]

    def back(parts, routes):
        return [lax.ppermute(part, "tm", reverse(route)) for part, route in zip(parts, routes)]

    edge_0 = answer(edge_asks, 0, True, ())
    edge_back_0 = back(edge_0, edge_routes)
    edge_1 = answer(edge_asks, 1, True, edge_0)
    edge_back_1 = back(edge_1, edge_routes)
    nears = [
        attend(after(q_parts[c], *edge_1), tiles[c][:2], True, True, jnp.float32, weight=0.01)
        for c in range(2)
    ]
    inner_0 = answer(inner_asks, 0, False, nears)
    inner_back_0 = back(inner_0, inner_routes)
    inner_1 = answer(inner_asks, 1, False, (*inner_0, *edge_back_1))
    inner_back_1 = back(inner_1, inner_routes)
    fars = [attend(after(q_parts[c], *inner_1), tiles[c][2:], False, True, jnp.float32) for c in range(2)]

    def joined(chunk, edge_back, inner_back, earlier):
        backs = [after(part, earlier) for pair in zip(edge_back, inner_back) for part in pair]
        mine, other = join((nears[chunk], fars[chunk], *backs), rows, steps, time_count)
        return mine, lax.ppermute(other, "tm", core_route)

    mine, other = joined(0, edge_back_0, inner_back_0, fars[1])
    total = project((mine, other), (False, True), weight, 0, None, jnp.float32)
    mine, other = joined(1, edge_back_1, inner_back_1, total)
    total = project((mine,), (False,), weight, middle, total, jnp.float32)
    return project((other,), (True,), weight, middle, total, jnp.bfloat16)


def solution(mesh):
    in_specs = (
        P(("parts", "tm"), None, None),
        P(("parts", "tm"), None, None),
        P(("parts", "tm"), None, None),
        P(),
    )
    out_specs = P(("parts", "tm"), None)
    return jax.shard_map(
        per_device, mesh=mesh, in_specs=in_specs, out_specs=out_specs, check_vma=False
    )
```

```python
import functools
import math

import jax
import jax.numpy as jnp
from jax import lax
from jax.experimental import pallas as pl
from jax.experimental.pallas import tpu as pltpu
from jax.sharding import PartitionSpec as P

TCOLS = 4
HD = 128
CHUNK_HEADS = 2
STAT_ROWS = 16
PROJECT_COLS = 512
EXP2_SCALE = HD ** (-0.5) * math.log2(math.e)
MASKED = -1e30
VMEM_BYTES = 32 * 1024 * 1024


def after(array, *earlier):
    return lax.optimization_barrier((array, *earlier))[0]


def dot_rows(a, b):
    return lax.dot_general(a, b, (((1,), (1,)), ((), ())), preferred_element_type=jnp.float32)


def stat_blocks(rows, width):
    return -(-rows // width)


def is_edge():
    col = (lax.axis_index("tm") // 2) % TCOLS
    return (col == 0) | (col == TCOLS - 1)


def attend_head(q_ref, tiles, cols):
    query = q_ref[:, cols]
    scores = [dot_rows(tile[0, :, cols], query) for tile in tiles]
    top = jnp.max(functools.reduce(jnp.maximum, scores), axis=0, keepdims=True)
    top = top.astype(jnp.bfloat16).astype(jnp.float32)
    total = jnp.zeros_like(top)
    out = jnp.zeros((HD, query.shape[0]), jnp.float32)
    for score, tile in zip(scores, tiles):
        probs = jnp.exp2((score - top) * EXP2_SCALE).astype(jnp.bfloat16)
        total += jnp.sum(probs.astype(jnp.float32), axis=0, keepdims=True)
        out += lax.dot_general(
            tile[1, :, cols], probs, (((0,), (0,)), ((), ())), preferred_element_type=jnp.float32
        )
    return top, total, out


def head_columns(width):
    return [slice(first, first + HD) for first in range(0, width, HD)]


def put_partial(heads, out_ref):
    width = out_ref.shape[1]
    rows = heads[0][0].shape[1]
    stats = []
    for cols, (top, total, out) in zip(head_columns(width), heads):
        high = total.astype(jnp.bfloat16).astype(jnp.float32)
        stats += [top, high, total - high]
        out_ref[:rows, cols] = out.T.astype(out_ref.dtype)
    stats.append(jnp.zeros((STAT_ROWS - len(stats), rows), jnp.float32))
    stats = jnp.concatenate(stats, axis=0)
    for block in range(stat_blocks(rows, width)):
        piece = stats[:, block * width : (block + 1) * width]
        if piece.shape[1] < width:
            piece = jnp.concatenate(
                (piece, jnp.zeros((STAT_ROWS, width - piece.shape[1]), jnp.float32)), axis=1
            )
        first = rows + block * STAT_ROWS
        out_ref[first : first + STAT_ROWS, :] = piece.astype(out_ref.dtype)


def edge_kernel(q_ref, own_ref, next_ref, out_ref):
    @pl.when(is_edge())
    def _():
        columns = head_columns(q_ref.shape[1])
        put_partial([attend_head(q_ref, (own_ref, next_ref), cols) for cols in columns], out_ref)


def near_kernel(everywhere, q_ref, own_ref, next_ref, state_ref):
    def attend():
        rows, width = q_ref.shape
        stats = []
        for cols in head_columns(width):
            top, total, out = attend_head(q_ref, (own_ref, next_ref), cols)
            state_ref[cols, :] = out
            stats += [top, total]
        stats.append(jnp.zeros((STAT_ROWS - len(stats), rows), jnp.float32))
        state_ref[width:, :] = jnp.concatenate(stats, axis=0)

    if everywhere:
        attend()
    else:
        pl.when(jnp.logical_not(is_edge()))(attend)


def finish_kernel(everywhere, q_ref, far_ref, state_ref, out_ref):
    width = q_ref.shape[1]

    def held():
        stats = state_ref[width:, :]
        return [
            (stats[2 * n : 2 * n + 1], stats[2 * n + 1 : 2 * n + 2], state_ref[cols, :])
            for n, cols in enumerate(head_columns(width))
        ]

    @pl.when(jnp.logical_not(is_edge()))
    def _():
        heads = []
        for cols, (top_0, total_0, out_0) in zip(head_columns(width), held()):
            top_1, total_1, out_1 = attend_head(q_ref, (far_ref,), cols)
            top = jnp.maximum(top_0, top_1)
            weight_0 = jnp.exp2((top_0 - top) * EXP2_SCALE)
            weight_1 = jnp.exp2((top_1 - top) * EXP2_SCALE)
            total = weight_0 * total_0 + weight_1 * total_1
            heads.append((top, total, weight_0 * out_0 + weight_1 * out_1))
        put_partial(heads, out_ref)

    if everywhere:
        pl.when(is_edge())(lambda: put_partial(held(), out_ref))


def partial_call(kernel, name, out_shape, dtype, tiles, weight, *args):
    rows, width = args[0].shape
    keys = tiles * rows
    return pl.pallas_call(
        kernel,
        out_shape=jax.ShapeDtypeStruct(out_shape, dtype),
        compiler_params=pltpu.CompilerParams(vmem_limit_bytes=VMEM_BYTES),
        cost_estimate=pl.CostEstimate(
            flops=int(weight * 4 * rows * keys * width),
            bytes_accessed=int(weight * 2 * width * (2 * rows + 2 * keys)),
            transcendentals=int(weight * rows * keys * width // HD),
        ),
        name=name,
    )(*args)


def partial_shape(query):
    rows, width = query.shape
    return rows + STAT_ROWS * stat_blocks(rows, width), width


def attend_edge(query, own, nxt):
    return partial_call(edge_kernel, "edge", partial_shape(query), jnp.bfloat16, 2, 1.0, query, own, nxt)


def attend_near(query, own, nxt, everywhere):
    rows, width = query.shape
    kernel = functools.partial(near_kernel, everywhere)
    return partial_call(kernel, "near", (width + STAT_ROWS, rows), jnp.float32, 2, 0.01, query, own, nxt)


def attend_far(query, far, state, everywhere, dtype):
    kernel = functools.partial(finish_kernel, everywhere)
    return partial_call(kernel, "far", partial_shape(query), dtype, 1, 1.0, query, far, state)


def join_kernel(steps, time_count, *refs):
    mine_ref, other_ref = refs[-2:]
    half, width = mine_ref.shape
    rows = 2 * half
    position = lax.axis_index("tm")
    group = position % 2
    time_tile = position // (2 * TCOLS)
    edge = is_edge()

    def load(ref, *index):
        at_edge, inner = ref
        value = at_edge[index].astype(jnp.float32)
        return value if inner is None else jnp.where(edge, value, inner[index].astype(jnp.float32))

    sources = [(refs[0], None)] + [refs[1 + 2 * n : 3 + 2 * n] for n in range(len(steps))]
    parts = []
    for ref, step in zip(sources, (0, *steps)):
        source = time_tile + step
        ok = None if step == 0 or time_count == 2 else (source >= 0) & (source < time_count)
        stats = [
            load(ref, slice(rows + block * STAT_ROWS, rows + (block + 1) * STAT_ROWS), slice(None))
            for block in range(stat_blocks(rows, width))
        ]
        stats = jnp.concatenate(stats, axis=1)[:, :rows].T
        parts.append((ref, stats, ok))
    for head in range(width // HD):
        cols = slice(head * HD, (head + 1) * HD)
        tops, sums = [], []
        for _, stats, ok in parts:
            top = stats[:, 3 * head : 3 * head + 1]
            tops.append(top if ok is None else jnp.where(ok, top, MASKED))
            sums.append(stats[:, 3 * head + 1 : 3 * head + 2] + stats[:, 3 * head + 2 : 3 * head + 3])
        top = functools.reduce(jnp.maximum, tops)
        weights = [jnp.exp2((t - top) * EXP2_SCALE) for t in tops]
        inverse = 1.0 / sum(w * s for w, s in zip(weights, sums))
        value = sum((w * inverse) * load(p[0], slice(rows), cols) for w, p in zip(weights, parts))
        value = value.astype(jnp.bfloat16)
        mine_ref[:, cols] = jnp.where(group == 0, value[:half], value[half:])
        other_ref[:, cols] = jnp.where(group == 0, value[half:], value[:half])


def join(parts, rows, steps, time_count):
    width = parts[0].shape[1]
    out = jax.ShapeDtypeStruct((rows // 2, width), jnp.bfloat16)
    return pl.pallas_call(
        functools.partial(join_kernel, steps, time_count),
        out_shape=(out, out),
        compiler_params=pltpu.CompilerParams(vmem_limit_bytes=VMEM_BYTES),
        cost_estimate=pl.CostEstimate(
            flops=8 * rows * width, bytes_accessed=10 * rows * width, transcendentals=0
        ),
        name="join",
    )(*parts)


def project_kernel(first, swaps, has_total, last, *refs):
    inputs, w_ref = refs[: len(swaps)], refs[len(swaps)]
    out_ref = refs[-2] if last else refs[-1]
    copies = []
    group = lax.axis_index("tm") % 2
    width = inputs[0].shape[1]
    model = w_ref.shape[2]
    block = PROJECT_COLS if model % PROJECT_COLS == 0 else model
    for start in range(0, model, block):
        cols = slice(start, start + block)
        result = refs[len(swaps) + 1][:, cols] if has_total else 0.0
        for ref, swap in zip(inputs, swaps):
            which = 1 - group if swap else group
            result += jnp.dot(
                ref[...], w_ref[which, first : first + width, cols], preferred_element_type=jnp.float32
            )
        out_ref[:, cols] = result.astype(out_ref.dtype)
        if last:
            home = refs[-3].at[:, cols]
            copies.append(pltpu.make_async_copy(out_ref.at[:, cols], home, refs[-1].at[len(copies)]))
            copies[-1].start()
    for copy in copies:
        copy.wait()


def project(inputs, swaps, weight, first, total, last):
    half, width = inputs[0].shape
    model = weight.shape[2]
    args = [*inputs, weight] if total is None else [*inputs, weight, total]
    dtype = jnp.bfloat16 if last else jnp.float32
    scratch = [pltpu.VMEM((half, model), dtype), pltpu.SemaphoreType.DMA((-(-model // PROJECT_COLS),))]
    return pl.pallas_call(
        functools.partial(project_kernel, first, swaps, total is not None, last),
        in_specs=[pl.BlockSpec(memory_space=pltpu.VMEM)] * len(args),
        out_specs=pl.BlockSpec(memory_space=pl.ANY if last else pltpu.VMEM),
        out_shape=jax.ShapeDtypeStruct((half, model), dtype),
        scratch_shapes=scratch if last else [],
        compiler_params=pltpu.CompilerParams(vmem_limit_bytes=VMEM_BYTES),
        cost_estimate=pl.CostEstimate(
            flops=2 * len(inputs) * half * width * model,
            bytes_accessed=2 * len(inputs) * width * model + 4 * half * model,
            transcendentals=0,
        ),
        name="project",
    )(*args)


def reverse(route):
    return [(b, a) for a, b in route]


def per_device(query_states, key_states, value_states, out_weight):
    query, key, value = query_states[0], key_states[0], value_states[0]
    rows, half_width = query.shape
    devices = lax.axis_size("tm")
    time_count = devices // (2 * TCOLS)
    places = range(devices)
    row = 2 * TCOLS

    def at_edge(place):
        return (place // 2) % TCOLS in (0, TCOLS - 1)

    next_route = [(p, p ^ 2) for p in places]
    far_route = [(p, p ^ 4) for p in places if at_edge(p)]
    across_route = [(p, p ^ 6) for p in places if not at_edge(p)]
    if time_count == 2:
        steps = (1,)
        ask_routes = [[(p, p ^ row) for p in places]]
    else:
        steps = (1, -1)
        ask_routes = [[(p, p + s * row) for p in places if 0 <= p + s * row < devices] for s in steps]
    edge_routes = [[pair for pair in route if at_edge(pair[0])] for route in ask_routes]
    inner_routes = [[pair for pair in route if not at_edge(pair[0])] for route in ask_routes]
    core_route = [(p, p ^ 1) for p in places]

    weight = out_weight.reshape(2, half_width, out_weight.shape[1])
    middle = half_width // HD // 2 * HD
    cuts = slice(0, middle), slice(middle, half_width)
    q_parts = [query[:, cut] for cut in cuts]
    own_0 = jnp.stack((key[:, cuts[0]], value[:, cuts[0]]))
    key, value = after((key, value), own_0)
    own_1 = jnp.stack((key[:, cuts[1]], value[:, cuts[1]]))

    edge_query = after(query, own_0)
    edge_asks = [lax.ppermute(edge_query, "tm", route) for route in edge_routes]
    next_0 = lax.ppermute(own_0, "tm", next_route)
    next_1 = lax.ppermute(own_1, "tm", next_route)
    inner_query = after(query, next_0)
    inner_asks = [lax.ppermute(inner_query, "tm", route) for route in inner_routes]
    far_0 = lax.ppermute(next_0, "tm", far_route)
    far_1 = lax.ppermute(after(own_1, next_0), "tm", across_route)
    nears = (own_0, next_0), (own_1, next_1)

    def back(parts, routes):
        return [lax.ppermute(part, "tm", reverse(route)) for part, route in zip(parts, routes)]

    edge_0 = [attend_edge(q[:, cuts[0]], *nears[0]) for q in edge_asks]
    edge_back_0 = back(edge_0, edge_routes)
    own_states = [attend_near(after(q_parts[0], *edge_0), *nears[0], True)]
    edge_1 = [attend_edge(after(q[:, cuts[1]], *edge_0, *own_states), *nears[1]) for q in edge_asks]
    edge_back_1 = back(edge_1, edge_routes)

    asked_0 = [after(q[:, cuts[0]], *own_states) for q in inner_asks]
    states_0 = [attend_near(q, *nears[0], False) for q in asked_0]
    asked_1 = [after(q[:, cuts[1]], *states_0) for q in inner_asks]
    states_1 = [attend_near(q, *nears[1], False) for q in asked_1]
    states_0 = [after(state, *states_1) for state in states_0]
    inner_0 = [attend_far(q, far_0, state, False, jnp.bfloat16) for q, state in zip(asked_0, states_0)]
    inner_back_0 = back(inner_0, inner_routes)
    states_1 = [after(state, *inner_0, *edge_back_1) for state in states_1]
    inner_1 = [attend_far(q, far_1, state, False, jnp.bfloat16) for q, state in zip(asked_1, states_1)]
    inner_back_1 = back(inner_1, inner_routes)
    own_states.append(attend_near(after(q_parts[1], *inner_1), *nears[1], True))
    owns = [
        attend_far(after(q_parts[c], *inner_1), far, own_states[c], True, jnp.float32)
        for c, far in enumerate((far_0, far_1))
    ]

    def joined(chunk, edge_back, inner_back, earlier):
        backs = [after(part, earlier) for pair in zip(edge_back, inner_back) for part in pair]
        mine, other = join((owns[chunk], *backs), rows, steps, time_count)
        return mine, lax.ppermute(other, "tm", core_route)

    mine, other = joined(0, edge_back_0, inner_back_0, owns[1])
    total = project((mine, other), (False, True), weight, 0, None, False)
    mine, other = joined(1, edge_back_1, inner_back_1, total)
    total = project((mine,), (False,), weight, middle, total, False)
    return project((other,), (True,), weight, middle, total, True)


def solution(mesh):
    in_specs = (
        P(("parts", "tm"), None, None),
        P(("parts", "tm"), None, None),
        P(("parts", "tm"), None, None),
        P(),
    )
    out_specs = P(("parts", "tm"), None)
    return jax.shard_map(
        per_device, mesh=mesh, in_specs=in_specs, out_specs=out_specs, check_vma=False
    )
```

```python
import functools
import math

import jax
import jax.numpy as jnp
from jax import lax
from jax.experimental import pallas as pl
from jax.experimental.pallas import tpu as pltpu
from jax.sharding import PartitionSpec as P

TCOLS = 4
HD = 128
CHUNK_HEADS = 2
STAT_ROWS = 16
PROJECT_COLS = 512
EXP2_SCALE = HD ** (-0.5) * math.log2(math.e)
MASKED = -1e30
VMEM_BYTES = 32 * 1024 * 1024


def after(array, *earlier):
    return lax.optimization_barrier((array, *earlier))[0]


def dot_rows(a, b):
    return lax.dot_general(a, b, (((1,), (1,)), ((), ())), preferred_element_type=jnp.float32)


def stat_blocks(rows, width):
    return -(-rows // width)


def is_edge():
    col = (lax.axis_index("tm") // 2) % TCOLS
    return (col == 0) | (col == TCOLS - 1)


def attend_head(q_ref, tiles, cols):
    query = q_ref[:, cols]
    scores = [dot_rows(tile[0, :, cols], query) for tile in tiles]
    top = jnp.max(functools.reduce(jnp.maximum, scores), axis=0, keepdims=True)
    top = top.astype(jnp.bfloat16).astype(jnp.float32)
    total = jnp.zeros_like(top)
    out = jnp.zeros((HD, query.shape[0]), jnp.float32)
    for score, tile in zip(scores, tiles):
        probs = jnp.exp2((score - top) * EXP2_SCALE).astype(jnp.bfloat16)
        total += jnp.sum(probs.astype(jnp.float32), axis=0, keepdims=True)
        out += lax.dot_general(
            tile[1, :, cols], probs, (((0,), (0,)), ((), ())), preferred_element_type=jnp.float32
        )
    return top, total, out


def head_columns(width):
    return [slice(first, first + HD) for first in range(0, width, HD)]


def put_partial(heads, out_ref):
    width = out_ref.shape[1]
    rows = heads[0][0].shape[1]
    stats = []
    for cols, (top, total, out) in zip(head_columns(width), heads):
        high = total.astype(jnp.bfloat16).astype(jnp.float32)
        stats += [top, high, total - high]
        out_ref[:rows, cols] = out.T.astype(out_ref.dtype)
    stats.append(jnp.zeros((STAT_ROWS - len(stats), rows), jnp.float32))
    stats = jnp.concatenate(stats, axis=0)
    for block in range(stat_blocks(rows, width)):
        piece = stats[:, block * width : (block + 1) * width]
        if piece.shape[1] < width:
            piece = jnp.concatenate(
                (piece, jnp.zeros((STAT_ROWS, width - piece.shape[1]), jnp.float32)), axis=1
            )
        first = rows + block * STAT_ROWS
        out_ref[first : first + STAT_ROWS, :] = piece.astype(out_ref.dtype)


def edge_kernel(q_ref, own_ref, next_ref, out_ref):
    @pl.when(is_edge())
    def _():
        columns = head_columns(q_ref.shape[1])
        put_partial([attend_head(q_ref, (own_ref, next_ref), cols) for cols in columns], out_ref)


def near_kernel(everywhere, q_ref, own_ref, next_ref, state_ref):
    def attend():
        rows, width = q_ref.shape
        stats = []
        for cols in head_columns(width):
            top, total, out = attend_head(q_ref, (own_ref, next_ref), cols)
            state_ref[cols, :] = out
            stats += [top, total]
        stats.append(jnp.zeros((STAT_ROWS - len(stats), rows), jnp.float32))
        state_ref[width:, :] = jnp.concatenate(stats, axis=0)

    if everywhere:
        attend()
    else:
        pl.when(jnp.logical_not(is_edge()))(attend)


def finish_kernel(everywhere, q_ref, far_ref, state_ref, out_ref):
    width = q_ref.shape[1]

    def held():
        stats = state_ref[width:, :]
        return [
            (stats[2 * n : 2 * n + 1], stats[2 * n + 1 : 2 * n + 2], state_ref[cols, :])
            for n, cols in enumerate(head_columns(width))
        ]

    @pl.when(jnp.logical_not(is_edge()))
    def _():
        heads = []
        for cols, (top_0, total_0, out_0) in zip(head_columns(width), held()):
            top_1, total_1, out_1 = attend_head(q_ref, (far_ref,), cols)
            top = jnp.maximum(top_0, top_1)
            weight_0 = jnp.exp2((top_0 - top) * EXP2_SCALE)
            weight_1 = jnp.exp2((top_1 - top) * EXP2_SCALE)
            total = weight_0 * total_0 + weight_1 * total_1
            heads.append((top, total, weight_0 * out_0 + weight_1 * out_1))
        put_partial(heads, out_ref)

    if everywhere:
        pl.when(is_edge())(lambda: put_partial(held(), out_ref))


def partial_call(kernel, name, out_shape, dtype, tiles, weight, *args):
    rows, width = args[0].shape
    keys = tiles * rows
    return pl.pallas_call(
        kernel,
        out_shape=jax.ShapeDtypeStruct(out_shape, dtype),
        compiler_params=pltpu.CompilerParams(vmem_limit_bytes=VMEM_BYTES),
        cost_estimate=pl.CostEstimate(
            flops=int(weight * 4 * rows * keys * width),
            bytes_accessed=int(weight * 2 * width * (2 * rows + 2 * keys)),
            transcendentals=int(weight * rows * keys * width // HD),
        ),
        name=name,
    )(*args)


def partial_shape(query):
    rows, width = query.shape
    return rows + STAT_ROWS * stat_blocks(rows, width), width


def attend_edge(query, own, nxt):
    return partial_call(edge_kernel, "edge", partial_shape(query), jnp.bfloat16, 2, 1.0, query, own, nxt)


def attend_near(query, own, nxt, everywhere):
    rows, width = query.shape
    kernel = functools.partial(near_kernel, everywhere)
    return partial_call(kernel, "near", (width + STAT_ROWS, rows), jnp.float32, 2, 0.01, query, own, nxt)


def attend_far(query, far, state, everywhere, dtype):
    kernel = functools.partial(finish_kernel, everywhere)
    return partial_call(kernel, "far", partial_shape(query), dtype, 1, 0.01, query, far, state)


def join_kernel(steps, time_count, *refs):
    mine_ref, other_ref = refs[-2:]
    half, width = mine_ref.shape
    rows = 2 * half
    position = lax.axis_index("tm")
    group = position % 2
    time_tile = position // (2 * TCOLS)
    edge = is_edge()

    def load(ref, *index):
        at_edge, inner = ref
        value = at_edge[index].astype(jnp.float32)
        return value if inner is None else jnp.where(edge, value, inner[index].astype(jnp.float32))

    sources = [(refs[0], None)] + [refs[1 + 2 * n : 3 + 2 * n] for n in range(len(steps))]
    parts = []
    for ref, step in zip(sources, (0, *steps)):
        source = time_tile + step
        ok = None if step == 0 or time_count == 2 else (source >= 0) & (source < time_count)
        stats = [
            load(ref, slice(rows + block * STAT_ROWS, rows + (block + 1) * STAT_ROWS), slice(None))
            for block in range(stat_blocks(rows, width))
        ]
        stats = jnp.concatenate(stats, axis=1)[:, :rows].T
        parts.append((ref, stats, ok))
    for head in range(width // HD):
        cols = slice(head * HD, (head + 1) * HD)
        tops, sums = [], []
        for _, stats, ok in parts:
            top = stats[:, 3 * head : 3 * head + 1]
            tops.append(top if ok is None else jnp.where(ok, top, MASKED))
            sums.append(stats[:, 3 * head + 1 : 3 * head + 2] + stats[:, 3 * head + 2 : 3 * head + 3])
        top = functools.reduce(jnp.maximum, tops)
        weights = [jnp.exp2((t - top) * EXP2_SCALE) for t in tops]
        inverse = 1.0 / sum(w * s for w, s in zip(weights, sums))
        value = sum((w * inverse) * load(p[0], slice(rows), cols) for w, p in zip(weights, parts))
        value = value.astype(jnp.bfloat16)
        mine_ref[:, cols] = jnp.where(group == 0, value[:half], value[half:])
        other_ref[:, cols] = jnp.where(group == 0, value[half:], value[:half])


def join(parts, rows, steps, time_count):
    width = parts[0].shape[1]
    out = jax.ShapeDtypeStruct((rows // 2, width), jnp.bfloat16)
    return pl.pallas_call(
        functools.partial(join_kernel, steps, time_count),
        out_shape=(out, out),
        compiler_params=pltpu.CompilerParams(vmem_limit_bytes=VMEM_BYTES),
        cost_estimate=pl.CostEstimate(
            flops=8 * rows * width, bytes_accessed=10 * rows * width, transcendentals=0
        ),
        name="join",
    )(*parts)


def project_kernel(first, swaps, has_total, last, *refs):
    inputs, w_ref = refs[: len(swaps)], refs[len(swaps)]
    out_ref = refs[-2] if last else refs[-1]
    copies = []
    group = lax.axis_index("tm") % 2
    width = inputs[0].shape[1]
    model = w_ref.shape[2]
    block = PROJECT_COLS if model % PROJECT_COLS == 0 else model
    for start in range(0, model, block):
        cols = slice(start, start + block)
        result = refs[len(swaps) + 1][:, cols] if has_total else 0.0
        for ref, swap in zip(inputs, swaps):
            which = 1 - group if swap else group
            result += jnp.dot(
                ref[...], w_ref[which, first : first + width, cols], preferred_element_type=jnp.float32
            )
        out_ref[:, cols] = result.astype(out_ref.dtype)
        if last:
            home = refs[-3].at[:, cols]
            copies.append(pltpu.make_async_copy(out_ref.at[:, cols], home, refs[-1].at[len(copies)]))
            copies[-1].start()
    for copy in copies:
        copy.wait()


def project(inputs, swaps, weight, first, total, last):
    half, width = inputs[0].shape
    model = weight.shape[2]
    args = [*inputs, weight] if total is None else [*inputs, weight, total]
    dtype = jnp.bfloat16 if last else jnp.float32
    scratch = [pltpu.VMEM((half, model), dtype), pltpu.SemaphoreType.DMA((-(-model // PROJECT_COLS),))]
    return pl.pallas_call(
        functools.partial(project_kernel, first, swaps, total is not None, last),
        in_specs=[pl.BlockSpec(memory_space=pltpu.VMEM)] * len(args),
        out_specs=pl.BlockSpec(memory_space=pl.ANY if last else pltpu.VMEM),
        out_shape=jax.ShapeDtypeStruct((half, model), dtype),
        scratch_shapes=scratch if last else [],
        compiler_params=pltpu.CompilerParams(vmem_limit_bytes=VMEM_BYTES),
        cost_estimate=pl.CostEstimate(
            flops=2 * len(inputs) * half * width * model,
            bytes_accessed=2 * len(inputs) * width * model + 4 * half * model,
            transcendentals=0,
        ),
        name="project",
    )(*args)


def reverse(route):
    return [(b, a) for a, b in route]


def per_device(query_states, key_states, value_states, out_weight):
    query, key, value = query_states[0], key_states[0], value_states[0]
    rows, half_width = query.shape
    devices = lax.axis_size("tm")
    time_count = devices // (2 * TCOLS)
    places = range(devices)
    row = 2 * TCOLS

    def at_edge(place):
        return (place // 2) % TCOLS in (0, TCOLS - 1)

    next_route = [(p, p ^ 2) for p in places]
    far_route = [(p, p ^ 4) for p in places if at_edge(p)]
    across_route = [(p, p ^ 6) for p in places if not at_edge(p)]
    if time_count == 2:
        steps = (1,)
        ask_routes = [[(p, p ^ row) for p in places]]
    else:
        steps = (1, -1)
        ask_routes = [[(p, p + s * row) for p in places if 0 <= p + s * row < devices] for s in steps]
    edge_routes = [[pair for pair in route if at_edge(pair[0])] for route in ask_routes]
    inner_routes = [[pair for pair in route if not at_edge(pair[0])] for route in ask_routes]
    core_route = [(p, p ^ 1) for p in places]

    weight = out_weight.reshape(2, half_width, out_weight.shape[1])
    middle = half_width // HD // 2 * HD
    cuts = slice(0, middle), slice(middle, half_width)
    q_parts = [query[:, cut] for cut in cuts]
    own_0 = jnp.stack((key[:, cuts[0]], value[:, cuts[0]]))
    key, value = after((key, value), own_0)
    own_1 = jnp.stack((key[:, cuts[1]], value[:, cuts[1]]))

    edge_query = after(query, own_0)
    edge_asks = [lax.ppermute(edge_query, "tm", route) for route in edge_routes]
    next_0 = lax.ppermute(own_0, "tm", next_route)
    next_1 = lax.ppermute(own_1, "tm", next_route)
    inner_query = after(query, next_0)
    inner_asks = [lax.ppermute(inner_query, "tm", route) for route in inner_routes]
    far_0 = lax.ppermute(next_0, "tm", far_route)
    far_1 = lax.ppermute(after(own_1, next_0), "tm", across_route)
    nears = (own_0, next_0), (own_1, next_1)

    def back(parts, routes):
        return [lax.ppermute(part, "tm", reverse(route)) for part, route in zip(parts, routes)]

    edge_0 = [attend_edge(q[:, cuts[0]], *nears[0]) for q in edge_asks]
    edge_back_0 = back(edge_0, edge_routes)
    own_states = [attend_near(after(q_parts[0], *edge_0), *nears[0], True)]
    edge_1 = [attend_edge(after(q[:, cuts[1]], *edge_0, *own_states), *nears[1]) for q in edge_asks]
    edge_back_1 = back(edge_1, edge_routes)

    asked_0 = [after(q[:, cuts[0]], *own_states) for q in inner_asks]
    states_0 = [attend_near(q, *nears[0], False) for q in asked_0]
    asked_1 = [after(q[:, cuts[1]], *states_0) for q in inner_asks]
    states_1 = [attend_near(q, *nears[1], False) for q in asked_1]
    states_0 = [after(state, *states_1) for state in states_0]
    inner_0 = [attend_far(q, far_0, state, False, jnp.bfloat16) for q, state in zip(asked_0, states_0)]
    inner_back_0 = back(inner_0, inner_routes)
    states_1 = [after(state, *inner_0, *edge_back_1) for state in states_1]
    inner_1 = [attend_far(q, far_1, state, False, jnp.bfloat16) for q, state in zip(asked_1, states_1)]
    inner_back_1 = back(inner_1, inner_routes)
    own_states.append(attend_near(after(q_parts[1], *inner_1), *nears[1], True))
    owns = [
        attend_far(after(q_parts[c], *inner_1), far, own_states[c], True, jnp.float32)
        for c, far in enumerate((far_0, far_1))
    ]

    def joined(chunk, edge_back, inner_back, earlier):
        backs = [after(part, earlier) for pair in zip(edge_back, inner_back) for part in pair]
        mine, other = join((owns[chunk], *backs), rows, steps, time_count)
        return mine, lax.ppermute(other, "tm", core_route)

    mine, other = joined(0, edge_back_0, inner_back_0, owns[1])
    total = project((mine, other), (False, True), weight, 0, None, False)
    mine, other = joined(1, edge_back_1, inner_back_1, total)
    total = project((mine,), (False,), weight, middle, total, False)
    return project((other,), (True,), weight, middle, total, True)


def solution(mesh):
    in_specs = (
        P(("parts", "tm"), None, None),
        P(("parts", "tm"), None, None),
        P(("parts", "tm"), None, None),
        P(),
    )
    out_specs = P(("parts", "tm"), None)
    return jax.shard_map(
        per_device, mesh=mesh, in_specs=in_specs, out_specs=out_specs, check_vma=False
    )
```
